128 devices in a mesh: ma: 8 (over y, x_hi), blk: 16 (over x_lo, z, core).
Axes of the slice: x: 4 (x_hi: 2, x_lo: 2; x = x_hi * 2 + x_lo), y: 4, z: 4, core: 2. Of those that a mesh axis runs over, the one named last changes fastest.
Arguments:
- cycle_rows: float32 [65536, 2048], P(('ma', 'blk')), may hold values from -6 to 6
- owner_map: int32 [16], replicated, may hold values from 0 to 15, each once
- factors: float32 [4, 16, 1024, 64, 128], P(None, 'ma', 'blk'), may hold values from -0.5 to 0.5
Outputs:
- coeffs: float32 [16, 1024, 64, 128], P('ma', 'blk')
The draws below stay inside these ranges and needn't reach their ends.
Inputs may be any that keep to these rules, and one draw needn't show every extreme that they name: owner_map is a permutation of the m-blocks; slot q of factors and of coeffs belongs to m-block owner_map[q].
All inputs are finite; a program needn't handle non-finite values.
Results may differ from the reference program's by a relative error of at most 0.0001.
Values sent between devices are 32-bit elements; how exact they have to be, the bound alone decides.
No kernel may reach another device: no remote copies, remote signals or barrier semaphores. Data moves between devices by JAX's collectives and lax.ppermute only.
A program may use at most 128 MiB of HBM per device.

```python
import jax
import jax.numpy as jnp
import numpy as np
from jax import lax

K = 64
G = 64
LEVELS = 4
CB = 128
RDEV = 512
CYCLES = 65536
MBLK = 16
COLS = 2048
N_MA = 8
N_BLK = 16


def shard_levels(own_key, extent, split, least, largest):
    level, own = 1.0, jax.random.fold_in(own_key, 6)
    for dim, blocks in split:
        steps = jnp.exp(jax.random.uniform(jax.random.fold_in(own, dim), (blocks,), jnp.float32, least / len(split), largest / len(split)))
        level = level * jnp.repeat(steps, extent[dim] // blocks).reshape([-1 if axis == dim else 1 for axis in range(len(extent))])
    return level


def centred(key, extent, width, bound, pieces=(), kind=jnp.bfloat16):
    loudness = shard_levels(key, extent, pieces, -0.22, 0.18) if pieces else 1.0
    result = jax.random.normal(key, extent, jnp.float32) * width * loudness
    return jnp.minimum(jnp.maximum(result, -bound), bound).astype(kind)


def setup_inputs(seed: int = 0) -> dict:
    splits = jax.random.split(jax.random.key(seed), 4)
    cycle_rows = centred(splits[0], (CYCLES, COLS), 1.0, 6.0, ((0, 128),), jnp.float32)
    owner_map = jax.random.permutation(splits[1], MBLK).astype(jnp.int32)
    factors = centred(splits[2], (LEVELS, MBLK, N_BLK * G, K, 2 * K), (2 * K) ** -0.5, 0.5, ((1, 8), (2, 16)), jnp.float32)
    return dict(cycle_rows=cycle_rows, owner_map=owner_map, factors=factors)


def reference(cycle_rows, owner_map, factors):
    shaped = cycle_rows.reshape(N_MA, N_BLK, RDEV, MBLK, CB)
    shaped = jnp.transpose(shaped, (3, 1, 0, 2, 4))
    ordered = jnp.take(shaped, owner_map, axis=0).reshape(MBLK, N_BLK * G, K, CB)
    bit_count = N_BLK.bit_length() - 1

    def one_block(slot_index):
        block_state = lax.dynamic_index_in_dim(ordered, slot_index, 0, keepdims=False)
        block_state = block_state.reshape(N_BLK, G, K, CB)
        slot_factors = lax.dynamic_index_in_dim(factors, slot_index, 1, keepdims=False)
        for level_index in range(LEVELS):
            partner_index = np.arange(N_BLK) ^ (1 << (level_index % bit_count))
            partner_state = block_state[partner_index]
            level_factor = slot_factors[level_index].reshape(N_BLK, G, K, 2 * K)
            stacked = jnp.concatenate([block_state, partner_state], axis=2)
            block_state = jnp.einsum("bgkj,bgjc->bgkc", level_factor, stacked,
                                     precision=lax.Precision.HIGHEST)
        return block_state.reshape(N_BLK * G, K, CB)

    coeffs = lax.map(one_block, jnp.arange(MBLK, dtype=jnp.int32))
    return coeffs
```

```python
import functools

import jax
import jax.numpy as jnp
from jax import lax
from jax.experimental import pallas as pl
from jax.experimental.pallas import tpu as pltpu
from jax.sharding import PartitionSpec as P


def permute_xor(x, axis, mask):
    return lax.ppermute(x, axis, [(i, i ^ mask) for i in range(lax.axis_size(axis))])


def pick_body(place, owner_map, rows, out):
    del place, owner_map
    out[0] = rows[...]


def pick_slots(place, owner_map, rows, part, local_slots, block_cols):
    cycle_count = rows.shape[0]

    def column(slot, place, owner_map):
        return 0, owner_map[(place[0] ^ part) * local_slots + slot]

    return pl.pallas_call(
        pick_body,
        grid_spec=pltpu.PrefetchScalarGridSpec(
            num_scalar_prefetch=2,
            grid=(local_slots,),
            in_specs=[pl.BlockSpec((cycle_count, block_cols), column)],
            out_specs=pl.BlockSpec(
                (1, cycle_count, block_cols), lambda slot, place, owner_map: (slot, 0, 0)
            ),
        ),
        out_shape=jax.ShapeDtypeStruct((local_slots, cycle_count, block_cols), rows.dtype),
        cost_estimate=pl.CostEstimate(
            flops=0, bytes_accessed=8 * local_slots * cycle_count * block_cols, transcendentals=0
        ),
        name="pick_slots",
    )(place, owner_map, rows)


def split(x):
    high = x.astype(jnp.bfloat16)
    return high, (x - high.astype(jnp.float32)).astype(jnp.bfloat16)


def block_product(factor, own, other):
    factor_high, factor_low = split(factor)
    high, low = split(jnp.concatenate([own, other], axis=0))
    dot = functools.partial(jnp.dot, preferred_element_type=jnp.float32)
    return dot(factor_high, high) + (dot(factor_high, low) + dot(factor_low, high))


def level_body(place, factors, own, other, *refs):
    del place
    out = refs[-1]
    for group in range(own.shape[1]):
        out[0, group] = block_product(factors[0, 0, group], own[0, group], other[0, group])


def level_product(place, factors, own, other, level, part, filled=None, whole=False):
    slots, groups, rank, cols = own.shape
    step = 4
    per = groups // step
    block = (1, step, rank, cols)

    def local(slot, g, place):
        return slot, g, 0, 0

    def placed(slot, g, place):
        return slot, (place[0] ^ part) * per + g, 0, 0

    operands = [place, factors, own, other]
    in_specs = [
        pl.BlockSpec(
            (1, 1, step, rank, factors.shape[-1]),
            lambda slot, g, place: (level,) + placed(slot, g, place),
        ),
        pl.BlockSpec(block, local),
        pl.BlockSpec(block, local),
    ]
    aliases = {}
    if filled is not None:
        operands.append(filled)
        in_specs.append(pl.BlockSpec(memory_space=pl.ANY))
        aliases = {4: 0}
    shape = (slots, factors.shape[2], rank, cols) if whole else own.shape
    size = slots * groups * rank * cols
    return pl.pallas_call(
        level_body,
        grid_spec=pltpu.PrefetchScalarGridSpec(
            num_scalar_prefetch=1,
            grid=(slots, per),
            in_specs=in_specs,
            out_specs=pl.BlockSpec(block, placed if whole else local),
        ),
        out_shape=jax.ShapeDtypeStruct(shape, own.dtype),
        input_output_aliases=aliases,
        cost_estimate=pl.CostEstimate(
            flops=3 * 2 * size * factors.shape[-1], bytes_accessed=16 * size, transcendentals=0
        ),
        name="level_product",
    )(*operands)


def on_device(cycle_rows, owner_map, factors):
    block_count = owner_map.shape[0]
    block_cols = cycle_rows.shape[1] // block_count
    level_count, local_slots, group_count, rank, _ = factors.shape
    parts = lax.axis_size("ma")
    bit_count = lax.axis_size("blk").bit_length() - 1
    place = jnp.reshape(lax.axis_index("ma"), (1,)).astype(jnp.int32)
    part_shape = (local_slots, group_count // parts, rank, block_cols)
    coeffs = None
    for part in range(parts):
        state = pick_slots(place, owner_map, cycle_rows, part, local_slots, block_cols)
        if part:
            state = permute_xor(state, "ma", part)
        state = state.reshape(part_shape)
        for level in range(level_count):
            other = permute_xor(state, "blk", 1 << (level % bit_count))
            last = level == level_count - 1
            state = level_product(
                place, factors, state, other, level, part, coeffs if last else None, last
            )
        coeffs = state
    return coeffs


def solution(mesh):
    placed = (P(("ma", "blk"), None), P(), P(None, "ma", "blk", None, None))
    return jax.shard_map(
        on_device, mesh=mesh, in_specs=placed, out_specs=P("ma", "blk", None, None), check_vma=False
    )
```

```python
import collections
import functools

import jax
import jax.numpy as jnp
from jax import lax
from jax.experimental import pallas as pl
from jax.experimental.pallas import tpu as pltpu
from jax.sharding import PartitionSpec as P

ANY = pl.BlockSpec(memory_space=pl.ANY)
VMEM = pl.BlockSpec(memory_space=pltpu.VMEM)
SCALARS = pl.BlockSpec(memory_space=pltpu.SMEM)
MARK = pltpu.VMEM((8, 128), jnp.float32)
FREE = pl.CostEstimate(flops=0, bytes_accessed=0, transcendentals=0)
PARAMS = pltpu.CompilerParams(vmem_limit_bytes=4 << 20)

Chunk = collections.namedtuple("Chunk", ["part", "slot", "slots", "group", "groups"])


def permute_xor(x, axis, mask):
    return lax.ppermute(x, axis, [(i, i ^ mask) for i in range(lax.axis_size(axis))])


def in_vmem(x):
    return pltpu.with_memory_space_constraint(x, pltpu.VMEM)


def in_hbm(x):
    return pltpu.with_memory_space_constraint(x, pltpu.HBM)


def call(body, operands, in_specs, outs, out_specs, token, name, scratch=(), aliases={}):
    tokens = [] if token is None else [token]
    return pl.pallas_call(
        body,
        in_specs=in_specs + [ANY] * len(tokens),
        out_specs=out_specs + [ANY],
        out_shape=outs + [MARK],
        scratch_shapes=list(scratch),
        input_output_aliases=aliases,
        cost_estimate=FREE,
        compiler_params=PARAMS,
        name=name,
    )(*operands, *tokens)


def run_copies(copies):
    for copy in copies:
        copy.start()
    for copy in copies:
        copy.wait()


def pick_body(chunks, local_slots, place, owner_map, rows, *refs):
    outs, sems = refs[-2 - len(chunks) : -2], refs[-1]
    copies = []
    for chunk, out in zip(chunks, outs):
        cols = out.shape[-1]
        for slot in range(chunk.slots):
            column = owner_map[(place[0] ^ chunk.part) * local_slots + chunk.slot + slot]
            start = pl.multiple_of(column * cols, cols)
            source = rows.at[pl.ds(chunk.group, chunk.groups), :, pl.ds(start, cols)]
            copies.append(pltpu.make_async_copy(source, out.at[slot], sems.at[len(copies)]))
    run_copies(copies)


def pick_slots(place, owner_map, rows, chunks, local_slots, block_cols, token):
    outs = [
        pltpu.VMEM((chunk.slots, chunk.groups, rows.shape[1], block_cols), rows.dtype)
        for chunk in chunks
    ]
    return call(
        functools.partial(pick_body, chunks, local_slots),
        [place, owner_map, in_hbm(rows)],
        [SCALARS, SCALARS, ANY],
        outs,
        [VMEM] * len(chunks),
        token,
        "pick_slots",
        [pltpu.SemaphoreType.DMA((sum(chunk.slots for chunk in chunks),))],
    )


def fetch_body(level, factors, *refs):
    out, sems = refs[-3], refs[-1]
    run_copies(
        [
            pltpu.make_async_copy(factors.at[level, slot], out.at[slot], sems.at[slot])
            for slot in range(out.shape[0])
        ]
    )


def fetch_factors(factors, level, token):
    return call(
        functools.partial(fetch_body, level),
        [in_hbm(factors)],
        [ANY],
        [pltpu.VMEM(factors.shape[1:], factors.dtype)],
        [VMEM],
        token,
        "fetch_factors",
        [pltpu.SemaphoreType.DMA((factors.shape[1],))],
    )


def gate_body(x, *refs):
    pass


def gate(x, token):
    return call(
        gate_body,
        [in_vmem(x)],
        [ANY],
        [pltpu.VMEM(x.shape, x.dtype)],
        [ANY],
        token,
        "gate",
        aliases={0: 0},
    )


def split(x):
    high = x.astype(jnp.bfloat16)
    return high, (x - high.astype(jnp.float32)).astype(jnp.bfloat16)


def block_product(factor, own, other):
    factor_high, factor_low = split(factor)
    high, low = split(jnp.concatenate([own, other], axis=0))
    dot = functools.partial(jnp.dot, preferred_element_type=jnp.float32)
    both = jnp.concatenate([factor_high, factor_low], axis=1)
    return dot(both, jnp.concatenate([high, high], axis=0)) + dot(factor_high, low)


def early_body(chunk, parts, place, factors, own, other, *refs):
    out, held, sem = refs[-4], refs[-2], refs[-1]
    first = (place[0] ^ chunk.part) * (factors.shape[2] // parts) + chunk.group
    source = factors.at[0, pl.ds(chunk.slot, chunk.slots), pl.ds(first, chunk.groups)]
    run_copies([pltpu.make_async_copy(source, held, sem)])
    for slot in range(chunk.slots):
        for group in range(chunk.groups):
            out[slot, group] = block_product(held[slot, group], own[slot, group], other[slot, group])


def early_product(place, factors, own, other, chunk, parts, token):
    held = own.shape[:3] + factors.shape[4:]
    return call(
        functools.partial(early_body, chunk, parts),
        [place, in_hbm(factors), in_vmem(own), in_vmem(other)],
        [SCALARS, ANY, VMEM, VMEM],
        [pltpu.VMEM(own.shape, own.dtype)],
        [VMEM],
        token,
        "early_product",
        [pltpu.VMEM(held, factors.dtype), pltpu.SemaphoreType.DMA],
    )


def level_body(chunk, parts, place, factors, own, other, *refs):
    out = refs[-2]
    first = (place[0] ^ chunk.part) * (factors.shape[1] // parts) + chunk.group
    for slot in range(chunk.slots):
        for group in range(chunk.groups):
            factor = factors[chunk.slot + slot, first + group]
            out[slot, group] = block_product(factor, own[slot, group], other[slot, group])


def level_product(place, factors, own, other, chunk, parts, token):
    return call(
        functools.partial(level_body, chunk, parts),
        [place, in_vmem(factors), in_vmem(own), in_vmem(other)],
        [SCALARS, VMEM, VMEM, VMEM],
        [pltpu.VMEM(own.shape, own.dtype)],
        [VMEM],
        token,
        "level_product",
    )


def last_body(chunk, parts, place, factors, own, other, *refs):
    out, held, sem = refs[-4], refs[-2], refs[-1]
    first = (place[0] ^ chunk.part) * (factors.shape[1] // parts) + chunk.group
    for slot in range(chunk.slots):
        for group in range(chunk.groups):
            factor = factors[chunk.slot + slot, first + group]
            held[slot, group] = block_product(factor, own[slot, group], other[slot, group])
    place_out = out.at[pl.ds(chunk.slot, chunk.slots), pl.ds(first, chunk.groups)]
    run_copies([pltpu.make_async_copy(held, place_out, sem)])


def last_product(place, factors, own, other, chunk, parts, token, coeffs):
    filled = [] if coeffs is None else [in_hbm(coeffs)]
    return call(
        functools.partial(last_body, chunk, parts),
        [place, in_vmem(factors), in_vmem(own), in_vmem(other)] + filled,
        [SCALARS, VMEM, VMEM, VMEM] + [ANY] * len(filled),
        [pltpu.HBM(factors.shape[:3] + own.shape[3:], own.dtype)],
        [ANY],
        token,
        "last_product",
        [pltpu.VMEM(own.shape, own.dtype), pltpu.SemaphoreType.DMA],
        {4: 0} if filled else {},
    )


def chunks_of(parts, slots, groups):
    order = [2, 6, 1, 3, 7, 4, 5] if parts == 8 else list(range(1, parts))
    whole = [Chunk(part, 0, slots, 0, groups) for part in [0] + order[:-1]]
    return whole + [Chunk(order[-1], slot, 1, 0, groups) for slot in range(slots)]


PICK_AT = (0, 0, 1, 3, 7, 8, 16, 20, 25)
FETCH_AT = (3, 4, 8, 12)


def on_device(cycle_rows, owner_map, factors):
    block_count = owner_map.shape[0]
    block_cols = cycle_rows.shape[1] // block_count
    level_count, local_slots, group_count, rank, _ = factors.shape
    parts = lax.axis_size("ma")
    bit_count = lax.axis_size("blk").bit_length() - 1
    place = jnp.reshape(lax.axis_index("ma"), (1,)).astype(jnp.int32)
    groups = group_count // parts
    rows = cycle_rows.reshape(groups, rank, cycle_rows.shape[1])
    chunks = chunks_of(parts, local_slots, groups)
    state, other, fetched = {}, {}, {}
    token, coeffs = None, None
    flying = collections.deque()

    def exchange(i, level):
        other[i] = permute_xor(state[i], "blk", 1 << (level % bit_count))
        flying.append((level, i))

    def fetch(level):
        nonlocal token
        if level not in fetched:
            fetched[level], token = fetch_factors(factors, level, token)
        return fetched[level]

    def pick(i):
        nonlocal token
        state[i], token = pick_slots(
            place, owner_map, rows, [chunks[i]], local_slots, block_cols, token
        )
        if chunks[i].part:
            state[i] = permute_xor(state[i], "ma", chunks[i].part)
            flying.append((-1, i))
        else:
            exchange(i, 0)

    def land(level, i):
        nonlocal token, coeffs
        if level < 0:
            state[i], token = gate(state[i], token)
        elif level == 0 and not chunks[i].part:
            state[i], token = early_product(
                place, factors, state[i], other[i], chunks[i], parts, token
            )
        elif level < level_count - 1:
            state[i], token = level_product(
                place, fetch(level), state[i], other[i], chunks[i], parts, token
            )
        else:
            coeffs, token = last_product(
                place, fetch(level), state[i], other[i], chunks[i], parts, token, coeffs
            )
            return
        exchange(i, level + 1)

    picks = sorted(zip(PICK_AT, range(len(chunks))))
    landed = 0
    while picks or flying:
        while picks and (picks[0][0] <= landed or not flying):
            pick(picks.pop(0)[1])
        for level in range(level_count):
            if FETCH_AT[level] <= landed:
                fetch(level)
        land(*flying.popleft())
        landed += 1
    return coeffs


def solution(mesh):
    placed = (P(("ma", "blk"), None), P(), P(None, "ma", "blk", None, None))
    return jax.shard_map(
        on_device, mesh=mesh, in_specs=placed, out_specs=P("ma", "blk", None, None), check_vma=False
    )
```

```python
import collections
import functools

import jax
import jax.numpy as jnp
from jax import lax
from jax.experimental import pallas as pl
from jax.experimental.pallas import tpu as pltpu
from jax.sharding import PartitionSpec as P

ANY = pl.BlockSpec(memory_space=pl.ANY)
VMEM = pl.BlockSpec(memory_space=pltpu.VMEM)
SCALARS = pl.BlockSpec(memory_space=pltpu.SMEM)
MARK = pltpu.VMEM((8, 128), jnp.float32)
FREE = pl.CostEstimate(flops=0, bytes_accessed=0, transcendentals=0)
PARAMS = pltpu.CompilerParams(vmem_limit_bytes=4 << 20)

Chunk = collections.namedtuple("Chunk", ["part", "slot", "slots", "group", "groups"])


def permute_xor(x, axis, mask):
    return lax.ppermute(x, axis, [(i, i ^ mask) for i in range(lax.axis_size(axis))])


def in_vmem(x):
    return pltpu.with_memory_space_constraint(x, pltpu.VMEM)


def in_hbm(x):
    return pltpu.with_memory_space_constraint(x, pltpu.HBM)


def call(body, operands, in_specs, outs, out_specs, token, name, scratch=(), aliases={}):
    tokens = [] if token is None else [token]
    return pl.pallas_call(
        body,
        in_specs=in_specs + [ANY] * len(tokens),
        out_specs=out_specs + [ANY],
        out_shape=outs + [MARK],
        scratch_shapes=list(scratch),
        input_output_aliases=aliases,
        cost_estimate=FREE,
        compiler_params=PARAMS,
        name=name,
    )(*operands, *tokens)


def run_copies(copies):
    for copy in copies:
        copy.start()
    for copy in copies:
        copy.wait()


def pick_body(chunks, local_slots, place, owner_map, rows, *refs):
    outs, sems = refs[-2 - len(chunks) : -2], refs[-1]
    copies = []
    for chunk, out in zip(chunks, outs):
        cols = out.shape[-1]
        for slot in range(chunk.slots):
            column = owner_map[(place[0] ^ chunk.part) * local_slots + chunk.slot + slot]
            start = pl.multiple_of(column * cols, cols)
            source = rows.at[pl.ds(chunk.group, chunk.groups), :, pl.ds(start, cols)]
            copies.append(pltpu.make_async_copy(source, out.at[slot], sems.at[len(copies)]))
    run_copies(copies)


def pick_slots(place, owner_map, rows, chunks, local_slots, block_cols, token):
    outs = [
        pltpu.VMEM((chunk.slots, chunk.groups, rows.shape[1], block_cols), rows.dtype)
        for chunk in chunks
    ]
    return call(
        functools.partial(pick_body, chunks, local_slots),
        [place, owner_map, in_hbm(rows)],
        [SCALARS, SCALARS, ANY],
        outs,
        [VMEM] * len(chunks),
        token,
        "pick_slots",
        [pltpu.SemaphoreType.DMA((sum(chunk.slots for chunk in chunks),))],
    )


def fetch_body(level, factors, *refs):
    out, sems = refs[-3], refs[-1]
    run_copies(
        [
            pltpu.make_async_copy(factors.at[level, slot], out.at[slot], sems.at[slot])
            for slot in range(out.shape[0])
        ]
    )


def fetch_factors(factors, level, token):
    return call(
        functools.partial(fetch_body, level),
        [in_hbm(factors)],
        [ANY],
        [pltpu.VMEM(factors.shape[1:], factors.dtype)],
        [VMEM],
        token,
        "fetch_factors",
        [pltpu.SemaphoreType.DMA((factors.shape[1],))],
    )


def borrow_body(level, chunk, parts, place, factors, *refs):
    out, sem = refs[-3], refs[-1]
    first = (place[0] ^ chunk.part) * (factors.shape[2] // parts) + chunk.group
    source = factors.at[level, pl.ds(chunk.slot, chunk.slots), pl.ds(first, chunk.groups)]
    run_copies([pltpu.make_async_copy(source, out, sem)])


def pick_factors(place, factors, level, chunk, parts, token):
    shape = (chunk.slots, chunk.groups) + factors.shape[3:]
    return call(
        functools.partial(borrow_body, level, chunk, parts),
        [place, in_hbm(factors)],
        [SCALARS, ANY],
        [pltpu.VMEM(shape, factors.dtype)],
        [VMEM],
        token,
        "pick_factors",
        [pltpu.SemaphoreType.DMA],
    )


def gate_body(x, *refs):
    pass


def gate(x, token):
    return call(
        gate_body,
        [in_vmem(x)],
        [ANY],
        [pltpu.VMEM(x.shape, x.dtype)],
        [ANY],
        token,
        "gate",
        aliases={0: 0},
    )


def split(x):
    high = x.astype(jnp.bfloat16)
    return high, (x - high.astype(jnp.float32)).astype(jnp.bfloat16)


def block_product(factor, own, other):
    factor_high, factor_low = split(factor)
    high, low = split(jnp.concatenate([own, other], axis=0))
    dot = functools.partial(jnp.dot, preferred_element_type=jnp.float32)
    both = jnp.concatenate([factor_high, factor_low], axis=1)
    return dot(both, jnp.concatenate([high, high], axis=0)) + dot(factor_high, low)


def early_body(chunk, parts, place, factors, own, other, *refs):
    out, held, sem = refs[-4], refs[-2], refs[-1]
    first = (place[0] ^ chunk.part) * (factors.shape[2] // parts) + chunk.group
    source = factors.at[0, pl.ds(chunk.slot, chunk.slots), pl.ds(first, chunk.groups)]
    run_copies([pltpu.make_async_copy(source, held, sem)])
    for slot in range(chunk.slots):
        for group in range(chunk.groups):
            out[slot, group] = block_product(held[slot, group], own[slot, group], other[slot, group])


def early_product(place, factors, own, other, chunk, parts, token):
    held = own.shape[:3] + factors.shape[4:]
    return call(
        functools.partial(early_body, chunk, parts),
        [place, in_hbm(factors), in_vmem(own), in_vmem(other)],
        [SCALARS, ANY, VMEM, VMEM],
        [pltpu.VMEM(own.shape, own.dtype)],
        [VMEM],
        token,
        "early_product",
        [pltpu.VMEM(held, factors.dtype), pltpu.SemaphoreType.DMA],
    )


def level_body(chunk, parts, place, factors, own, other, *refs):
    out = refs[-2]
    first = (place[0] ^ chunk.part) * (factors.shape[1] // parts) + chunk.group
    for slot in range(chunk.slots):
        for group in range(chunk.groups):
            factor = factors[chunk.slot + slot, first + group]
            out[slot, group] = block_product(factor, own[slot, group], other[slot, group])


def level_product(place, factors, own, other, chunk, parts, token):
    return call(
        functools.partial(level_body, chunk, parts),
        [place, in_vmem(factors), in_vmem(own), in_vmem(other)],
        [SCALARS, VMEM, VMEM, VMEM],
        [pltpu.VMEM(own.shape, own.dtype)],
        [VMEM],
        token,
        "level_product",
    )


def both_body(chunk, parts, place, factors, lent, own, other, *refs):
    out, partner_out = refs[-3], refs[-2]
    first = (place[0] ^ chunk.part) * (factors.shape[1] // parts) + chunk.group
    for slot in range(chunk.slots):
        for group in range(chunk.groups):
            factor = factors[chunk.slot + slot, first + group]
            mine, theirs = own[slot, group], other[slot, group]
            out[slot, group] = block_product(factor, mine, theirs)
            partner_out[slot, group] = block_product(lent[slot, group], theirs, mine)


def both_products(place, factors, lent, own, other, chunk, parts, token):
    shape = pltpu.VMEM(own.shape, own.dtype)
    return call(
        functools.partial(both_body, chunk, parts),
        [place, in_vmem(factors), in_vmem(lent), in_vmem(own), in_vmem(other)],
        [SCALARS, VMEM, VMEM, VMEM, VMEM],
        [shape, shape],
        [VMEM, VMEM],
        token,
        "both_products",
    )


def last_body(chunk, parts, place, factors, own, other, *refs):
    out, held, sem = refs[-4], refs[-2], refs[-1]
    first = (place[0] ^ chunk.part) * (factors.shape[1] // parts) + chunk.group
    for slot in range(chunk.slots):
        for group in range(chunk.groups):
            factor = factors[chunk.slot + slot, first + group]
            held[slot, group] = block_product(factor, own[slot, group], other[slot, group])
    place_out = out.at[pl.ds(chunk.slot, chunk.slots), pl.ds(first, chunk.groups)]
    run_copies([pltpu.make_async_copy(held, place_out, sem)])


def last_product(place, factors, own, other, chunk, parts, token, coeffs):
    filled = [] if coeffs is None else [in_hbm(coeffs)]
    return call(
        functools.partial(last_body, chunk, parts),
        [place, in_vmem(factors), in_vmem(own), in_vmem(other)] + filled,
        [SCALARS, VMEM, VMEM, VMEM] + [ANY] * len(filled),
        [pltpu.HBM(factors.shape[:3] + own.shape[3:], own.dtype)],
        [ANY],
        token,
        "last_product",
        [pltpu.VMEM(own.shape, own.dtype), pltpu.SemaphoreType.DMA],
        {4: 0} if filled else {},
    )


ORDER = (0, 2, 1, 6, 3, 4, 7, 5)
CUTS = {5: (2, 2)}

PICK, LAND, SEND, FETCH, LEND = range(5)
PLAN = (
    (PICK, 0), (LEND, 0), (PICK, 1), (PICK, 2), LAND, (SEND, 0), (PICK, 3), LAND, (FETCH, 1), LAND, (LEND, 1),
    (PICK, 4), LAND, (FETCH, 0), (FETCH, 3), LAND, LAND, LAND, (SEND, 1), (FETCH, 2), LAND, (PICK, 5), LAND,
    LAND, (SEND, 2), LAND, LAND, LAND, (SEND, 3), LAND, LAND, (PICK, 6), LAND, LAND, LAND, (PICK, 7),
    (SEND, 4), LAND, LAND, LAND, LAND, (SEND, 5), (PICK, 8), LAND, LAND, LAND, LAND, LAND, (SEND, 6), LAND,
    LAND, LAND, LAND, LAND, LAND, (SEND, 7), LAND, LAND, LAND, LAND, (SEND, 8), LAND, LAND, LAND, LAND, LAND,
    LAND, LAND, LAND, LAND,
)


def pieces(part, slots, groups, sizes):
    cut, slot, group = [], 0, 0
    for size in sizes:
        blocks = slots * groups // size
        if blocks == slots * groups:
            return [Chunk(part, 0, slots, 0, groups)]
        cut.append(Chunk(part, slot, 1, group, blocks))
        slot, group = (slot, group + blocks) if group + blocks < groups else (slot + 1, 0)
    return cut


def chunks_of(parts, slots, groups):
    cut = []
    for part in ORDER:
        cut += pieces(part, slots, groups, CUTS.get(part, (1,)))
    return cut


def on_device(cycle_rows, owner_map, factors):
    block_count = owner_map.shape[0]
    block_cols = cycle_rows.shape[1] // block_count
    level_count, local_slots, group_count, rank, _ = factors.shape
    parts = lax.axis_size("ma")
    bit_count = lax.axis_size("blk").bit_length() - 1
    place = jnp.reshape(lax.axis_index("ma"), (1,)).astype(jnp.int32)
    groups = group_count // parts
    rows = cycle_rows.reshape(groups, rank, cycle_rows.shape[1])
    chunks = chunks_of(parts, local_slots, groups)
    state, other, fetched, lent = {}, {}, {}, {}
    token, coeffs = None, None
    flying = collections.deque()

    def exchange(i, level):
        other[i] = permute_xor(state[i], "blk", 1 << (level % bit_count))
        flying.append((level, i))

    def fetch(level):
        nonlocal token
        if level not in fetched:
            fetched[level], token = fetch_factors(factors, level, token)
        return fetched[level]

    def pick(i):
        nonlocal token
        state[i], token = pick_slots(
            place, owner_map, rows, [chunks[i]], local_slots, block_cols, token
        )
        if chunks[i].part:
            state[i] = permute_xor(state[i], "ma", chunks[i].part)
            flying.append((-1, i))
        else:
            exchange(i, 0)

    def lend(i):
        nonlocal token
        lent[i], token = pick_factors(place, factors, 1, chunks[i], parts, token)
        lent[i] = permute_xor(lent[i], "blk", 1 << (1 % bit_count))
        flying.append((-2, i))

    def land(level, i):
        nonlocal token, coeffs
        if level == -2:
            lent[i], token = gate(lent[i], token)
            return
        if level == 1 and i in lent:
            state[i], theirs, token = both_products(
                place, fetch(1), lent.pop(i), state[i], other[i], chunks[i], parts, token
            )
            bits = (1 << (1 % bit_count)) ^ (1 << (2 % bit_count))
            other[i] = permute_xor(theirs, "blk", bits)
            flying.append((2, i))
            return
        if level < 0:
            state[i], token = gate(state[i], token)
        elif level == 0 and not chunks[i].part:
            state[i], token = early_product(
                place, factors, state[i], other[i], chunks[i], parts, token
            )
        elif level < level_count - 1:
            state[i], token = level_product(
                place, fetch(level), state[i], other[i], chunks[i], parts, token
            )
        else:
            coeffs, token = last_product(
                place, fetch(level), state[i], other[i], chunks[i], parts, token, coeffs
            )
            return
        if level == 0:
            ready.append(i)
        else:
            exchange(i, level + 1)

    def send(i):
        nonlocal token
        if ready[-1] != i or not fresh:
            state[i], token = gate(state[i], token)
        ready.remove(i)
        exchange(i, 1)

    ready, fresh = [], False
    for step in PLAN:
        if step == LAND:
            level, i = flying.popleft()
            land(level, i)
            fresh = level == 0
        else:
            what, i = step
            {PICK: pick, SEND: send, FETCH: fetch, LEND: lend}[what](i)
            fresh = False
    return coeffs


def solution(mesh):
    placed = (P(("ma", "blk"), None), P(), P(None, "ma", "blk", None, None))
    return jax.shard_map(
        on_device, mesh=mesh, in_specs=placed, out_specs=P("ma", "blk", None, None), check_vma=False
    )
```

```python
import collections
import functools

import jax
import jax.numpy as jnp
from jax import lax
from jax.experimental import pallas as pl
from jax.experimental.pallas import tpu as pltpu
from jax.sharding import PartitionSpec as P

ANY = pl.BlockSpec(memory_space=pl.ANY)
VMEM = pl.BlockSpec(memory_space=pltpu.VMEM)
SCALARS = pl.BlockSpec(memory_space=pltpu.SMEM)
MARK = pltpu.VMEM((8, 128), jnp.float32)
FREE = pl.CostEstimate(flops=0, bytes_accessed=0, transcendentals=0)
PARAMS = pltpu.CompilerParams(vmem_limit_bytes=4 << 20)

Chunk = collections.namedtuple("Chunk", ["part", "slot", "slots", "group", "groups"])


def permute_xor(x, axis, mask):
    return lax.ppermute(x, axis, [(i, i ^ mask) for i in range(lax.axis_size(axis))])


def in_vmem(x):
    return pltpu.with_memory_space_constraint(x, pltpu.VMEM)


def in_hbm(x):
    return pltpu.with_memory_space_constraint(x, pltpu.HBM)


def call(body, operands, in_specs, outs, out_specs, token, name, scratch=(), aliases={}):
    tokens = [] if token is None else [token]
    return pl.pallas_call(
        body,
        in_specs=in_specs + [ANY] * len(tokens),
        out_specs=out_specs + [ANY],
        out_shape=outs + [MARK],
        scratch_shapes=list(scratch),
        input_output_aliases=aliases,
        cost_estimate=FREE,
        compiler_params=PARAMS,
        name=name,
    )(*operands, *tokens)


def run_copies(copies):
    for copy in copies:
        copy.start()
    for copy in copies:
        copy.wait()


def pick_body(chunks, local_slots, place, owner_map, rows, *refs):
    outs, sems = refs[-2 - len(chunks) : -2], refs[-1]
    copies = []
    for chunk, out in zip(chunks, outs):
        cols = out.shape[-1]
        for slot in range(chunk.slots):
            column = owner_map[(place[0] ^ chunk.part) * local_slots + chunk.slot + slot]
            start = pl.multiple_of(column * cols, cols)
            source = rows.at[pl.ds(chunk.group, chunk.groups), :, pl.ds(start, cols)]
            copies.append(pltpu.make_async_copy(source, out.at[slot], sems.at[len(copies)]))
    run_copies(copies)


def pick_slots(place, owner_map, rows, chunks, local_slots, block_cols, token):
    outs = [
        pltpu.VMEM((chunk.slots, chunk.groups, rows.shape[1], block_cols), rows.dtype)
        for chunk in chunks
    ]
    return call(
        functools.partial(pick_body, chunks, local_slots),
        [place, owner_map, in_hbm(rows)],
        [SCALARS, SCALARS, ANY],
        outs,
        [VMEM] * len(chunks),
        token,
        "pick_slots",
        [pltpu.SemaphoreType.DMA((sum(chunk.slots for chunk in chunks),))],
    )


def fetch_body(level, factors, *refs):
    out, sems = refs[-3], refs[-1]
    run_copies(
        [
            pltpu.make_async_copy(factors.at[level, slot], out.at[slot], sems.at[slot])
            for slot in range(out.shape[0])
        ]
    )


def fetch_factors(factors, level, token):
    return call(
        functools.partial(fetch_body, level),
        [in_hbm(factors)],
        [ANY],
        [pltpu.VMEM(factors.shape[1:], factors.dtype)],
        [VMEM],
        token,
        "fetch_factors",
        [pltpu.SemaphoreType.DMA((factors.shape[1],))],
    )


def borrow_body(level, chunk, parts, place, factors, *refs):
    out, sem = refs[-3], refs[-1]
    first = (place[0] ^ chunk.part) * (factors.shape[2] // parts) + chunk.group
    source = factors.at[level, pl.ds(chunk.slot, chunk.slots), pl.ds(first, chunk.groups)]
    run_copies([pltpu.make_async_copy(source, out, sem)])


def pick_factors(place, factors, level, chunk, parts, token):
    shape = (chunk.slots, chunk.groups) + factors.shape[3:]
    return call(
        functools.partial(borrow_body, level, chunk, parts),
        [place, in_hbm(factors)],
        [SCALARS, ANY],
        [pltpu.VMEM(shape, factors.dtype)],
        [VMEM],
        token,
        "pick_factors",
        [pltpu.SemaphoreType.DMA],
    )


def gate_body(x, *refs):
    pass


def gate(x, token):
    return call(
        gate_body,
        [in_vmem(x)],
        [ANY],
        [pltpu.VMEM(x.shape, x.dtype)],
        [ANY],
        token,
        "gate",
        aliases={0: 0},
    )


def split(x):
    high = x.astype(jnp.bfloat16)
    return high, (x - high.astype(jnp.float32)).astype(jnp.bfloat16)


def block_product(factor, own, other):
    factor_high, factor_low = split(factor)
    high, low = split(jnp.concatenate([own, other], axis=0))
    dot = functools.partial(jnp.dot, preferred_element_type=jnp.float32)
    both = jnp.concatenate([factor_high, factor_low], axis=1)
    return dot(both, jnp.concatenate([high, high], axis=0)) + dot(factor_high, low)


def early_body(chunk, parts, place, factors, own, other, *refs):
    out, held, sem = refs[-4], refs[-2], refs[-1]
    first = (place[0] ^ chunk.part) * (factors.shape[2] // parts) + chunk.group
    source = factors.at[0, pl.ds(chunk.slot, chunk.slots), pl.ds(first, chunk.groups)]
    run_copies([pltpu.make_async_copy(source, held, sem)])
    for slot in range(chunk.slots):
        for group in range(chunk.groups):
            out[slot, group] = block_product(held[slot, group], own[slot, group], other[slot, group])


def early_product(place, factors, own, other, chunk, parts, token):
    held = own.shape[:3] + factors.shape[4:]
    return call(
        functools.partial(early_body, chunk, parts),
        [place, in_hbm(factors), in_vmem(own), in_vmem(other)],
        [SCALARS, ANY, VMEM, VMEM],
        [pltpu.VMEM(own.shape, own.dtype)],
        [VMEM],
        token,
        "early_product",
        [pltpu.VMEM(held, factors.dtype), pltpu.SemaphoreType.DMA],
    )


def level_body(chunk, parts, place, factors, own, other, *refs):
    out = refs[-2]
    first = (place[0] ^ chunk.part) * (factors.shape[1] // parts) + chunk.group
    for slot in range(chunk.slots):
        for group in range(chunk.groups):
            factor = factors[chunk.slot + slot, first + group]
            out[slot, group] = block_product(factor, own[slot, group], other[slot, group])


def level_product(place, factors, own, other, chunk, parts, token):
    return call(
        functools.partial(level_body, chunk, parts),
        [place, in_vmem(factors), in_vmem(own), in_vmem(other)],
        [SCALARS, VMEM, VMEM, VMEM],
        [pltpu.VMEM(own.shape, own.dtype)],
        [VMEM],
        token,
        "level_product",
    )


def both_body(chunk, parts, place, factors, lent, own, other, *refs):
    out, partner_out = refs[-3], refs[-2]
    first = (place[0] ^ chunk.part) * (factors.shape[1] // parts) + chunk.group
    for slot in range(chunk.slots):
        for group in range(chunk.groups):
            factor = factors[chunk.slot + slot, first + group]
            mine, theirs = own[slot, group], other[slot, group]
            out[slot, group] = block_product(factor, mine, theirs)
            partner_out[slot, group] = block_product(lent[slot, group], theirs, mine)


def both_products(place, factors, lent, own, other, chunk, parts, token):
    shape = pltpu.VMEM(own.shape, own.dtype)
    return call(
        functools.partial(both_body, chunk, parts),
        [place, in_vmem(factors), in_vmem(lent), in_vmem(own), in_vmem(other)],
        [SCALARS, VMEM, VMEM, VMEM, VMEM],
        [shape, shape],
        [VMEM, VMEM],
        token,
        "both_products",
    )


def last_body(chunk, parts, place, factors, own, other, *refs):
    out, held, sem = refs[-4], refs[-2], refs[-1]
    first = (place[0] ^ chunk.part) * (factors.shape[1] // parts) + chunk.group
    for slot in range(chunk.slots):
        for group in range(chunk.groups):
            factor = factors[chunk.slot + slot, first + group]
            held[slot, group] = block_product(factor, own[slot, group], other[slot, group])
    place_out = out.at[pl.ds(chunk.slot, chunk.slots), pl.ds(first, chunk.groups)]
    run_copies([pltpu.make_async_copy(held, place_out, sem)])


def last_product(place, factors, own, other, chunk, parts, token, coeffs):
    filled = [] if coeffs is None else [in_hbm(coeffs)]
    return call(
        functools.partial(last_body, chunk, parts),
        [place, in_vmem(factors), in_vmem(own), in_vmem(other)] + filled,
        [SCALARS, VMEM, VMEM, VMEM] + [ANY] * len(filled),
        [pltpu.HBM(factors.shape[:3] + own.shape[3:], own.dtype)],
        [ANY],
        token,
        "last_product",
        [pltpu.VMEM(own.shape, own.dtype), pltpu.SemaphoreType.DMA],
        {4: 0} if filled else {},
    )


ORDER = (0, 2, 1, 6, 3, 4, 7, 5)
CUTS = {5: (2, 2)}

PICK, ADMIT, LEND, BORROW, FETCH = range(-5, 0)
PLAN = (
    (LEND, 0), (PICK, 1), (LEND, 1), (PICK, 0), (PICK, 3), (PICK, 4), (LEND, 2), (PICK, 2), (BORROW, 0),
    (FETCH, 0), (ADMIT, 1), (0, 0), (PICK, 5), (BORROW, 1), (FETCH, 1), (ADMIT, 3), (0, 1), (1, 0),
    (ADMIT, 4), (ADMIT, 2), (FETCH, 3), (0, 3), (FETCH, 2), (BORROW, 2), (PICK, 6), (PICK, 8), (1, 1),
    (ADMIT, 5), (2, 0), (0, 4), (1, 3), (0, 2), (3, 0), (1, 4), (2, 1), (ADMIT, 6), (0, 5), (1, 2), (PICK, 7),
    (ADMIT, 8), (2, 3), (0, 6), (0, 8), (1, 5), (2, 2), (ADMIT, 7), (3, 1), (2, 4), (3, 3), (1, 6), (3, 2),
    (2, 5), (1, 8), (0, 7), (3, 4), (2, 6), (1, 7), (2, 8), (3, 5), (2, 7), (3, 6), (3, 8), (3, 7),
)


def pieces(part, slots, groups, sizes):
    cut, slot, group = [], 0, 0
    for size in sizes:
        blocks = slots * groups // size
        if blocks == slots * groups:
            return [Chunk(part, 0, slots, 0, groups)]
        cut.append(Chunk(part, slot, 1, group, blocks))
        slot, group = (slot, group + blocks) if group + blocks < groups else (slot + 1, 0)
    return cut


def chunks_of(parts, slots, groups):
    cut = []
    for part in ORDER:
        cut += pieces(part, slots, groups, CUTS.get(part, (1,)))
    return cut


def on_device(cycle_rows, owner_map, factors):
    block_count = owner_map.shape[0]
    block_cols = cycle_rows.shape[1] // block_count
    level_count, local_slots, group_count, rank, _ = factors.shape
    parts = lax.axis_size("ma")
    bit_count = lax.axis_size("blk").bit_length() - 1
    place = jnp.reshape(lax.axis_index("ma"), (1,)).astype(jnp.int32)
    groups = group_count // parts
    rows = cycle_rows.reshape(groups, rank, cycle_rows.shape[1])
    chunks = chunks_of(parts, local_slots, groups)
    state, other, fetched, lent = {}, {}, {}, {}
    token, coeffs = None, None

    def start(i, mask):
        other[i] = permute_xor(state[i], "blk", mask)

    def mask_of(level):
        return 1 << (level % bit_count)

    def pick(i):
        nonlocal token
        chunk = chunks[i]
        state[i], token = pick_slots(
            place, owner_map, rows, [chunk], local_slots, block_cols, token
        )
        if chunk.part:
            state[i] = permute_xor(state[i], "ma", chunk.part)
        else:
            start(i, mask_of(0))

    def admit(i):
        nonlocal token
        state[i], token = gate(state[i], token)
        start(i, mask_of(0))

    def lend(i):
        nonlocal token
        lent[i], token = pick_factors(place, factors, 1, chunks[i], parts, token)
        lent[i] = permute_xor(lent[i], "blk", mask_of(1))

    def borrow(i):
        nonlocal token
        lent[i], token = gate(lent[i], token)

    def fetch(level):
        nonlocal token
        fetched[level], token = fetch_factors(factors, level, token)

    def product(level, i):
        nonlocal token, coeffs
        if level == level_count - 1:
            coeffs, token = last_product(
                place, fetched[level], state[i], other[i], chunks[i], parts, token, coeffs
            )
        elif level == 1 and i in lent:
            state[i], theirs, token = both_products(
                place, fetched[1], lent.pop(i), state[i], other[i], chunks[i], parts, token
            )
            other[i] = permute_xor(theirs, "blk", mask_of(1) ^ mask_of(2))
        else:
            if level == 0 and not chunks[i].part:
                state[i], token = early_product(
                    place, factors, state[i], other[i], chunks[i], parts, token
                )
            else:
                state[i], token = level_product(
                    place, fetched[level], state[i], other[i], chunks[i], parts, token
                )
            start(i, mask_of(level + 1))

    steps = {PICK: pick, ADMIT: admit, LEND: lend, BORROW: borrow, FETCH: fetch}
    for what, i in PLAN:
        if what in steps:
            steps[what](i)
        else:
            product(what, i)
    return coeffs


def solution(mesh):
    placed = (P(("ma", "blk"), None), P(), P(None, "ma", "blk", None, None))
    return jax.shard_map(
        on_device, mesh=mesh, in_specs=placed, out_specs=P("ma", "blk", None, None), check_vma=False
    )
```

```python
import collections
import functools

import jax
import jax.numpy as jnp
from jax import lax
from jax.experimental import pallas as pl
from jax.experimental.pallas import tpu as pltpu
from jax.sharding import PartitionSpec as P

ANY = pl.BlockSpec(memory_space=pl.ANY)
VMEM = pl.BlockSpec(memory_space=pltpu.VMEM)
SCALARS = pl.BlockSpec(memory_space=pltpu.SMEM)
MARK = pltpu.VMEM((8, 128), jnp.float32)
FREE = pl.CostEstimate(flops=0, bytes_accessed=0, transcendentals=0)
PARAMS = pltpu.CompilerParams(vmem_limit_bytes=4 << 20)

Chunk = collections.namedtuple("Chunk", ["part", "slot", "slots", "group", "groups"])


def permute_xor(x, axis, mask):
    return lax.ppermute(x, axis, [(i, i ^ mask) for i in range(lax.axis_size(axis))])


def in_vmem(x):
    return pltpu.with_memory_space_constraint(x, pltpu.VMEM)


def in_hbm(x):
    return pltpu.with_memory_space_constraint(x, pltpu.HBM)


def call(body, operands, in_specs, outs, out_specs, token, name, scratch=(), aliases={}):
    tokens = [] if token is None else [token]
    return pl.pallas_call(
        body,
        in_specs=in_specs + [ANY] * len(tokens),
        out_specs=out_specs + [ANY],
        out_shape=outs + [MARK],
        scratch_shapes=list(scratch),
        input_output_aliases=aliases,
        cost_estimate=FREE,
        compiler_params=PARAMS,
        name=name,
    )(*operands, *tokens)


def run_copies(copies):
    for copy in copies:
        copy.start()
    for copy in copies:
        copy.wait()


def pick_body(chunks, local_slots, place, owner_map, rows, *refs):
    outs, sems = refs[-2 - len(chunks) : -2], refs[-1]
    copies = []
    for chunk, out in zip(chunks, outs):
        cols = out.shape[-1]
        for slot in range(chunk.slots):
            column = owner_map[(place[0] ^ chunk.part) * local_slots + chunk.slot + slot]
            start = pl.multiple_of(column * cols, cols)
            source = rows.at[pl.ds(chunk.group, chunk.groups), :, pl.ds(start, cols)]
            copies.append(pltpu.make_async_copy(source, out.at[slot], sems.at[len(copies)]))
    run_copies(copies)


def pick_slots(place, owner_map, rows, chunks, local_slots, block_cols, token):
    outs = [
        pltpu.VMEM((chunk.slots, chunk.groups, rows.shape[1], block_cols), rows.dtype)
        for chunk in chunks
    ]
    return call(
        functools.partial(pick_body, chunks, local_slots),
        [place, owner_map, in_hbm(rows)],
        [SCALARS, SCALARS, ANY],
        outs,
        [VMEM] * len(chunks),
        token,
        "pick_slots",
        [pltpu.SemaphoreType.DMA((sum(chunk.slots for chunk in chunks),))],
    )


def fetch_body(level, factors, *refs):
    out, sems = refs[-3], refs[-1]
    run_copies(
        [
            pltpu.make_async_copy(factors.at[level, slot], out.at[slot], sems.at[slot])
            for slot in range(out.shape[0])
        ]
    )


def fetch_factors(factors, level, token):
    return call(
        functools.partial(fetch_body, level),
        [in_hbm(factors)],
        [ANY],
        [pltpu.VMEM(factors.shape[1:], factors.dtype)],
        [VMEM],
        token,
        "fetch_factors",
        [pltpu.SemaphoreType.DMA((factors.shape[1],))],
    )


def borrow_body(level, chunk, parts, place, factors, *refs):
    out, sem = refs[-3], refs[-1]
    first = (place[0] ^ chunk.part) * (factors.shape[2] // parts) + chunk.group
    source = factors.at[level, pl.ds(chunk.slot, chunk.slots), pl.ds(first, chunk.groups)]
    run_copies([pltpu.make_async_copy(source, out, sem)])


def pick_factors(place, factors, level, chunk, parts, token):
    shape = (chunk.slots, chunk.groups) + factors.shape[3:]
    return call(
        functools.partial(borrow_body, level, chunk, parts),
        [place, in_hbm(factors)],
        [SCALARS, ANY],
        [pltpu.VMEM(shape, factors.dtype)],
        [VMEM],
        token,
        "pick_factors",
        [pltpu.SemaphoreType.DMA],
    )


def gate_body(x, *refs):
    pass


def gate(x, token):
    return call(
        gate_body,
        [in_vmem(x)],
        [ANY],
        [pltpu.VMEM(x.shape, x.dtype)],
        [ANY],
        token,
        "gate",
        aliases={0: 0},
    )


def split(x):
    high = x.astype(jnp.bfloat16)
    return high, (x - high.astype(jnp.float32)).astype(jnp.bfloat16)


def block_product(factor, own, other):
    factor_high, factor_low = split(factor)
    high, low = split(jnp.concatenate([own, other], axis=0))
    dot = functools.partial(jnp.dot, preferred_element_type=jnp.float32)
    both = jnp.concatenate([factor_high, factor_low], axis=1)
    return dot(both, jnp.concatenate([high, high], axis=0)) + dot(factor_high, low)


def early_body(chunk, parts, place, factors, own, other, *refs):
    out, held, sem = refs[-4], refs[-2], refs[-1]
    first = (place[0] ^ chunk.part) * (factors.shape[2] // parts) + chunk.group
    source = factors.at[0, pl.ds(chunk.slot, chunk.slots), pl.ds(first, chunk.groups)]
    run_copies([pltpu.make_async_copy(source, held, sem)])
    for slot in range(chunk.slots):
        for group in range(chunk.groups):
            out[slot, group] = block_product(held[slot, group], own[slot, group], other[slot, group])


def early_product(place, factors, own, other, chunk, parts, token):
    held = own.shape[:3] + factors.shape[4:]
    return call(
        functools.partial(early_body, chunk, parts),
        [place, in_hbm(factors), in_vmem(own), in_vmem(other)],
        [SCALARS, ANY, VMEM, VMEM],
        [pltpu.VMEM(own.shape, own.dtype)],
        [VMEM],
        token,
        "early_product",
        [pltpu.VMEM(held, factors.dtype), pltpu.SemaphoreType.DMA],
    )


def level_body(chunk, parts, place, factors, own, other, *refs):
    out = refs[-2]
    first = (place[0] ^ chunk.part) * (factors.shape[1] // parts) + chunk.group
    for slot in range(chunk.slots):
        for group in range(chunk.groups):
            factor = factors[chunk.slot + slot, first + group]
            out[slot, group] = block_product(factor, own[slot, group], other[slot, group])


def level_product(place, factors, own, other, chunk, parts, token):
    return call(
        functools.partial(level_body, chunk, parts),
        [place, in_vmem(factors), in_vmem(own), in_vmem(other)],
        [SCALARS, VMEM, VMEM, VMEM],
        [pltpu.VMEM(own.shape, own.dtype)],
        [VMEM],
        token,
        "level_product",
    )


def both_body(chunk, parts, place, factors, lent, own, other, *refs):
    out, partner_out = refs[-3], refs[-2]
    first = (place[0] ^ chunk.part) * (factors.shape[1] // parts) + chunk.group
    for slot in range(chunk.slots):
        for group in range(chunk.groups):
            factor = factors[chunk.slot + slot, first + group]
            mine, theirs = own[slot, group], other[slot, group]
            out[slot, group] = block_product(factor, mine, theirs)
            partner_out[slot, group] = block_product(lent[slot, group], theirs, mine)


def both_products(place, factors, lent, own, other, chunk, parts, token):
    shape = pltpu.VMEM(own.shape, own.dtype)
    return call(
        functools.partial(both_body, chunk, parts),
        [place, in_vmem(factors), in_vmem(lent), in_vmem(own), in_vmem(other)],
        [SCALARS, VMEM, VMEM, VMEM, VMEM],
        [shape, shape],
        [VMEM, VMEM],
        token,
        "both_products",
    )


def last_body(chunk, parts, place, factors, own, other, *refs):
    out, held, sems = refs[-4], refs[-2], refs[-1]
    first = (place[0] ^ chunk.part) * (factors.shape[1] // parts) + chunk.group
    copies = []
    for slot in range(chunk.slots):
        for half in range(2):
            begin, count = half * chunk.groups // 2, chunk.groups // 2
            for group in range(begin, begin + count):
                factor = factors[chunk.slot + slot, first + group]
                held[slot, group] = block_product(factor, own[slot, group], other[slot, group])
            target = out.at[chunk.slot + slot, pl.ds(first + begin, count)]
            source = held.at[slot, pl.ds(begin, count)]
            copies.append(pltpu.make_async_copy(source, target, sems.at[len(copies)]))
            copies[-1].start()
    for copy in copies:
        copy.wait()


def last_product(place, factors, own, other, chunk, parts, token, coeffs):
    filled = [] if coeffs is None else [in_hbm(coeffs)]
    return call(
        functools.partial(last_body, chunk, parts),
        [place, in_vmem(factors), in_vmem(own), in_vmem(other)] + filled,
        [SCALARS, VMEM, VMEM, VMEM] + [ANY] * len(filled),
        [pltpu.HBM(factors.shape[:3] + own.shape[3:], own.dtype)],
        [ANY],
        token,
        "last_product",
        [pltpu.VMEM(own.shape, own.dtype), pltpu.SemaphoreType.DMA((2 * chunk.slots,))],
        {4: 0} if filled else {},
    )


ORDER = (0, 2, 1, 6, 3, 4, 7, 5)
CUTS = {5: (2, 2)}

PICK, ADMIT, LEND, BORROW, FETCH = range(-5, 0)
PLAN = (
    (LEND, 0), (PICK, 1), (LEND, 1), (PICK, 0), (PICK, 3), (PICK, 4), (LEND, 2), (PICK, 2), (BORROW, 0),
    (FETCH, 0), (ADMIT, 1), (0, 0), (PICK, 5), (BORROW, 1), (FETCH, 1), (ADMIT, 3), (0, 1), (1, 0),
    (ADMIT, 4), (ADMIT, 2), (FETCH, 3), (0, 3), (FETCH, 2), (BORROW, 2), (PICK, 6), (PICK, 8), (1, 1),
    (ADMIT, 5), (2, 0), (0, 4), (1, 3), (0, 2), (3, 0), (1, 4), (2, 1), (ADMIT, 6), (0, 5), (PICK, 7), (1, 2),
    (ADMIT, 8), (2, 3), (3, 1), (0, 6), (1, 5), (ADMIT, 7), (2, 2), (2, 4), (3, 3), (0, 7), (1, 6), (3, 4),
    (2, 5), (3, 2), (2, 6), (0, 8), (1, 7), (3, 5), (1, 8), (2, 7), (3, 6), (2, 8), (3, 7), (3, 8),
)


def pieces(part, slots, groups, sizes):
    cut, slot, group = [], 0, 0
    for size in sizes:
        blocks = slots * groups // size
        if blocks == slots * groups:
            return [Chunk(part, 0, slots, 0, groups)]
        cut.append(Chunk(part, slot, 1, group, blocks))
        slot, group = (slot, group + blocks) if group + blocks < groups else (slot + 1, 0)
    return cut


def chunks_of(parts, slots, groups):
    cut = []
    for part in ORDER:
        cut += pieces(part, slots, groups, CUTS.get(part, (1,)))
    return cut


def on_device(cycle_rows, owner_map, factors):
    block_count = owner_map.shape[0]
    block_cols = cycle_rows.shape[1] // block_count
    level_count, local_slots, group_count, rank, _ = factors.shape
    parts = lax.axis_size("ma")
    bit_count = lax.axis_size("blk").bit_length() - 1
    place = jnp.reshape(lax.axis_index("ma"), (1,)).astype(jnp.int32)
    groups = group_count // parts
    rows = cycle_rows.reshape(groups, rank, cycle_rows.shape[1])
    chunks = chunks_of(parts, local_slots, groups)
    state, other, fetched, lent = {}, {}, {}, {}
    token, coeffs = None, None

    def start(i, mask):
        other[i] = permute_xor(state[i], "blk", mask)

    def mask_of(level):
        return 1 << (level % bit_count)

    def pick(i):
        nonlocal token
        chunk = chunks[i]
        state[i], token = pick_slots(
            place, owner_map, rows, [chunk], local_slots, block_cols, token
        )
        if chunk.part:
            state[i] = permute_xor(state[i], "ma", chunk.part)
        else:
            start(i, mask_of(0))

    def admit(i):
        nonlocal token
        state[i], token = gate(state[i], token)
        start(i, mask_of(0))

    def lend(i):
        nonlocal token
        lent[i], token = pick_factors(place, factors, 1, chunks[i], parts, token)
        lent[i] = permute_xor(lent[i], "blk", mask_of(1))

    def borrow(i):
        nonlocal token
        lent[i], token = gate(lent[i], token)

    def fetch(level):
        nonlocal token
        fetched[level], token = fetch_factors(factors, level, token)

    def product(level, i):
        nonlocal token, coeffs
        if level == level_count - 1:
            coeffs, token = last_product(
                place, fetched[level], state[i], other[i], chunks[i], parts, token, coeffs
            )
        elif level == 1 and i in lent:
            state[i], theirs, token = both_products(
                place, fetched[1], lent.pop(i), state[i], other[i], chunks[i], parts, token
            )
            other[i] = permute_xor(theirs, "blk", mask_of(1) ^ mask_of(2))
        else:
            if level == 0 and not chunks[i].part:
                state[i], token = early_product(
                    place, factors, state[i], other[i], chunks[i], parts, token
                )
            else:
                state[i], token = level_product(
                    place, fetched[level], state[i], other[i], chunks[i], parts, token
                )
            start(i, mask_of(level + 1))

    steps = {PICK: pick, ADMIT: admit, LEND: lend, BORROW: borrow, FETCH: fetch}
    for what, i in PLAN:
        if what in steps:
            steps[what](i)
        else:
            product(what, i)
    return coeffs


def solution(mesh):
    placed = (P(("ma", "blk"), None), P(), P(None, "ma", "blk", None, None))
    return jax.shard_map(
        on_device, mesh=mesh, in_specs=placed, out_specs=P("ma", "blk", None, None), check_vma=False
    )
```

```python
import collections
import functools

import jax
import jax.numpy as jnp
from jax import lax
from jax.experimental import pallas as pl
from jax.experimental.pallas import tpu as pltpu
from jax.sharding import PartitionSpec as P

ANY = pl.BlockSpec(memory_space=pl.ANY)
VMEM = pl.BlockSpec(memory_space=pltpu.VMEM)
SCALARS = pl.BlockSpec(memory_space=pltpu.SMEM)
MARK = pltpu.VMEM((8, 128), jnp.float32)
FREE = pl.CostEstimate(flops=0, bytes_accessed=0, transcendentals=0)
PARAMS = pltpu.CompilerParams(vmem_limit_bytes=4 << 20)

Chunk = collections.namedtuple("Chunk", ["part", "slot", "slots", "group", "groups"])


def permute_xor(x, axis, mask):
    return lax.ppermute(x, axis, [(i, i ^ mask) for i in range(lax.axis_size(axis))])


def in_vmem(x):
    return pltpu.with_memory_space_constraint(x, pltpu.VMEM)


def in_hbm(x):
    return pltpu.with_memory_space_constraint(x, pltpu.HBM)


def call(body, operands, in_specs, outs, out_specs, token, name, scratch=(), aliases={}):
    tokens = [] if token is None else [token]
    return pl.pallas_call(
        body,
        in_specs=in_specs + [ANY] * len(tokens),
        out_specs=out_specs + [ANY],
        out_shape=outs + [MARK],
        scratch_shapes=list(scratch),
        input_output_aliases=aliases,
        cost_estimate=FREE,
        compiler_params=PARAMS,
        name=name,
    )(*operands, *tokens)


def run_copies(copies):
    for copy in copies:
        copy.start()
    for copy in copies:
        copy.wait()


def pick_body(chunks, local_slots, place, owner_map, rows, *refs):
    outs, sems = refs[-2 - len(chunks) : -2], refs[-1]
    copies = []
    for chunk, out in zip(chunks, outs):
        cols = out.shape[-1]
        for slot in range(chunk.slots):
            column = owner_map[(place[0] ^ chunk.part) * local_slots + chunk.slot + slot]
            start = pl.multiple_of(column * cols, cols)
            source = rows.at[pl.ds(chunk.group, chunk.groups), :, pl.ds(start, cols)]
            copies.append(pltpu.make_async_copy(source, out.at[slot], sems.at[len(copies)]))
    run_copies(copies)


def pick_slots(place, owner_map, rows, chunks, local_slots, block_cols, token):
    outs = [
        pltpu.VMEM((chunk.slots, chunk.groups, rows.shape[1], block_cols), rows.dtype)
        for chunk in chunks
    ]
    return call(
        functools.partial(pick_body, chunks, local_slots),
        [place, owner_map, in_hbm(rows)],
        [SCALARS, SCALARS, ANY],
        outs,
        [VMEM] * len(chunks),
        token,
        "pick_slots",
        [pltpu.SemaphoreType.DMA((sum(chunk.slots for chunk in chunks),))],
    )


def fetch_body(level, factors, *refs):
    out, sems = refs[-3], refs[-1]
    run_copies(
        [
            pltpu.make_async_copy(factors.at[level, slot], out.at[slot], sems.at[slot])
            for slot in range(out.shape[0])
        ]
    )


def fetch_factors(factors, level, token):
    return call(
        functools.partial(fetch_body, level),
        [in_hbm(factors)],
        [ANY],
        [pltpu.VMEM(factors.shape[1:], factors.dtype)],
        [VMEM],
        token,
        "fetch_factors",
        [pltpu.SemaphoreType.DMA((factors.shape[1],))],
    )


def borrow_body(level, chunk, parts, place, factors, *refs):
    out, sem = refs[-3], refs[-1]
    first = (place[0] ^ chunk.part) * (factors.shape[2] // parts) + chunk.group
    source = factors.at[level, pl.ds(chunk.slot, chunk.slots), pl.ds(first, chunk.groups)]
    run_copies([pltpu.make_async_copy(source, out, sem)])


def pick_factors(place, factors, level, chunk, parts, token):
    shape = (chunk.slots, chunk.groups) + factors.shape[3:]
    return call(
        functools.partial(borrow_body, level, chunk, parts),
        [place, in_hbm(factors)],
        [SCALARS, ANY],
        [pltpu.VMEM(shape, factors.dtype)],
        [VMEM],
        token,
        "pick_factors",
        [pltpu.SemaphoreType.DMA],
    )


def gate_body(x, *refs):
    pass


def gate(x, token):
    return call(
        gate_body,
        [in_vmem(x)],
        [ANY],
        [pltpu.VMEM(x.shape, x.dtype)],
        [ANY],
        token,
        "gate",
        aliases={0: 0},
    )


def split(x):
    high = x.astype(jnp.bfloat16)
    return high, (x - high.astype(jnp.float32)).astype(jnp.bfloat16)


def block_product(factor, own, other):
    factor_high, factor_low = split(factor)
    high, low = split(jnp.concatenate([own, other], axis=0))
    dot = functools.partial(jnp.dot, preferred_element_type=jnp.float32)
    both = jnp.concatenate([factor_high, factor_low], axis=1)
    return dot(both, jnp.concatenate([high, high], axis=0)) + dot(factor_high, low)


def early_body(chunk, parts, place, factors, own, other, *refs):
    out, held, sem = refs[-4], refs[-2], refs[-1]
    first = (place[0] ^ chunk.part) * (factors.shape[2] // parts) + chunk.group
    source = factors.at[0, pl.ds(chunk.slot, chunk.slots), pl.ds(first, chunk.groups)]
    run_copies([pltpu.make_async_copy(source, held, sem)])
    for slot in range(chunk.slots):
        for group in range(chunk.groups):
            out[slot, group] = block_product(held[slot, group], own[slot, group], other[slot, group])


def early_product(place, factors, own, other, chunk, parts, token):
    held = own.shape[:3] + factors.shape[4:]
    return call(
        functools.partial(early_body, chunk, parts),
        [place, in_hbm(factors), in_vmem(own), in_vmem(other)],
        [SCALARS, ANY, VMEM, VMEM],
        [pltpu.VMEM(own.shape, own.dtype)],
        [VMEM],
        token,
        "early_product",
        [pltpu.VMEM(held, factors.dtype), pltpu.SemaphoreType.DMA],
    )


def level_body(chunk, parts, place, factors, own, other, *refs):
    out = refs[-2]
    first = (place[0] ^ chunk.part) * (factors.shape[1] // parts) + chunk.group
    for slot in range(chunk.slots):
        for group in range(chunk.groups):
            factor = factors[chunk.slot + slot, first + group]
            out[slot, group] = block_product(factor, own[slot, group], other[slot, group])


def level_product(place, factors, own, other, chunk, parts, token):
    return call(
        functools.partial(level_body, chunk, parts),
        [place, in_vmem(factors), in_vmem(own), in_vmem(other)],
        [SCALARS, VMEM, VMEM, VMEM],
        [pltpu.VMEM(own.shape, own.dtype)],
        [VMEM],
        token,
        "level_product",
    )


def both_body(chunk, parts, place, factors, lent, own, other, *refs):
    out, partner_out = refs[-3], refs[-2]
    first = (place[0] ^ chunk.part) * (factors.shape[1] // parts) + chunk.group
    for slot in range(chunk.slots):
        for group in range(chunk.groups):
            factor = factors[chunk.slot + slot, first + group]
            mine, theirs = own[slot, group], other[slot, group]
            out[slot, group] = block_product(factor, mine, theirs)
            partner_out[slot, group] = block_product(lent[slot, group], theirs, mine)


def both_products(place, factors, lent, own, other, chunk, parts, token):
    shape = pltpu.VMEM(own.shape, own.dtype)
    return call(
        functools.partial(both_body, chunk, parts),
        [place, in_vmem(factors), in_vmem(lent), in_vmem(own), in_vmem(other)],
        [SCALARS, VMEM, VMEM, VMEM, VMEM],
        [shape, shape],
        [VMEM, VMEM],
        token,
        "both_products",
    )


def last_body(chunk, parts, place, factors, own, other, *refs):
    out, held, sems = refs[-4], refs[-2], refs[-1]
    first = (place[0] ^ chunk.part) * (factors.shape[1] // parts) + chunk.group
    copies = []
    for slot in range(chunk.slots):
        for half in range(2):
            begin, count = half * chunk.groups // 2, chunk.groups // 2
            for group in range(begin, begin + count):
                factor = factors[chunk.slot + slot, first + group]
                held[slot, group] = block_product(factor, own[slot, group], other[slot, group])
            target = out.at[chunk.slot + slot, pl.ds(first + begin, count)]
            source = held.at[slot, pl.ds(begin, count)]
            copies.append(pltpu.make_async_copy(source, target, sems.at[len(copies)]))
            copies[-1].start()
    for copy in copies:
        copy.wait()


def last_product(place, factors, own, other, chunk, parts, token, coeffs):
    filled = [] if coeffs is None else [in_hbm(coeffs)]
    return call(
        functools.partial(last_body, chunk, parts),
        [place, in_vmem(factors), in_vmem(own), in_vmem(other)] + filled,
        [SCALARS, VMEM, VMEM, VMEM] + [ANY] * len(filled),
        [pltpu.HBM(factors.shape[:3] + own.shape[3:], own.dtype)],
        [ANY],
        token,
        "last_product",
        [pltpu.VMEM(own.shape, own.dtype), pltpu.SemaphoreType.DMA((2 * chunk.slots,))],
        {4: 0} if filled else {},
    )


ORDER = (0, 2, 1, 6, 3, 4, 7, 5)
CUTS = {5: (2, 2)}

PICK, ADMIT, LEND, BORROW, FETCH = range(-5, 0)
PLAN = (
    (LEND, 0), (PICK, 1), (LEND, 1), (PICK, 0), (PICK, 3), (PICK, 4), (LEND, 2), (PICK, 2), (BORROW, 0),
    (FETCH, 0), (ADMIT, 1), (0, 0), (PICK, 5), (BORROW, 1), (FETCH, 1), (ADMIT, 3), (0, 1), (1, 0),
    (ADMIT, 4), (ADMIT, 2), (FETCH, 3), (0, 3), (FETCH, 2), (BORROW, 2), (PICK, 6), (PICK, 8), (1, 1),
    (ADMIT, 5), (2, 0), (0, 4), (1, 3), (0, 2), (3, 0), (1, 4), (2, 1), (ADMIT, 6), (0, 5), (1, 2), (PICK, 7),
    (ADMIT, 8), (2, 3), (0, 6), (0, 8), (1, 5), (2, 2), (ADMIT, 7), (3, 1), (2, 4), (3, 3), (1, 6), (3, 2),
    (2, 5), (1, 8), (0, 7), (3, 4), (2, 6), (1, 7), (2, 8), (3, 5), (2, 7), (3, 6), (3, 8), (3, 7),
)


def pieces(part, slots, groups, sizes):
    cut, slot, group = [], 0, 0
    for size in sizes:
        blocks = slots * groups // size
        if blocks == slots * groups:
            return [Chunk(part, 0, slots, 0, groups)]
        cut.append(Chunk(part, slot, 1, group, blocks))
        slot, group = (slot, group + blocks) if group + blocks < groups else (slot + 1, 0)
    return cut


def chunks_of(parts, slots, groups):
    cut = []
    for part in ORDER:
        cut += pieces(part, slots, groups, CUTS.get(part, (1,)))
    return cut


def on_device(cycle_rows, owner_map, factors):
    block_count = owner_map.shape[0]
    block_cols = cycle_rows.shape[1] // block_count
    level_count, local_slots, group_count, rank, _ = factors.shape
    parts = lax.axis_size("ma")
    bit_count = lax.axis_size("blk").bit_length() - 1
    place = jnp.reshape(lax.axis_index("ma"), (1,)).astype(jnp.int32)
    groups = group_count // parts
    rows = cycle_rows.reshape(groups, rank, cycle_rows.shape[1])
    chunks = chunks_of(parts, local_slots, groups)
    state, other, fetched, lent = {}, {}, {}, {}
    token, coeffs = None, None

    def start(i, mask):
        other[i] = permute_xor(state[i], "blk", mask)

    def mask_of(level):
        return 1 << (level % bit_count)

    def pick(i):
        nonlocal token
        chunk = chunks[i]
        state[i], token = pick_slots(
            place, owner_map, rows, [chunk], local_slots, block_cols, token
        )
        if chunk.part:
            state[i] = permute_xor(state[i], "ma", chunk.part)
        else:
            start(i, mask_of(0))

    def admit(i):
        nonlocal token
        state[i], token = gate(state[i], token)
        start(i, mask_of(0))

    def lend(i):
        nonlocal token
        lent[i], token = pick_factors(place, factors, 1, chunks[i], parts, token)
        lent[i] = permute_xor(lent[i], "blk", mask_of(1))

    def borrow(i):
        nonlocal token
        lent[i], token = gate(lent[i], token)

    def fetch(level):
        nonlocal token
        fetched[level], token = fetch_factors(factors, level, token)

    def product(level, i):
        nonlocal token, coeffs
        if level == level_count - 1:
            coeffs, token = last_product(
                place, fetched[level], state[i], other[i], chunks[i], parts, token, coeffs
            )
        elif level == 1 and i in lent:
            state[i], theirs, token = both_products(
                place, fetched[1], lent.pop(i), state[i], other[i], chunks[i], parts, token
            )
            other[i] = permute_xor(theirs, "blk", mask_of(1) ^ mask_of(2))
        else:
            if level == 0 and level not in fetched:
                state[i], token = early_product(
                    place, factors, state[i], other[i], chunks[i], parts, token
                )
            else:
                state[i], token = level_product(
                    place, fetched[level], state[i], other[i], chunks[i], parts, token
                )
            start(i, mask_of(level + 1))

    steps = {PICK: pick, ADMIT: admit, LEND: lend, BORROW: borrow, FETCH: fetch}
    for what, i in PLAN:
        if what in steps:
            steps[what](i)
        else:
            product(what, i)
    return coeffs


def solution(mesh):
    placed = (P(("ma", "blk"), None), P(), P(None, "ma", "blk", None, None))
    return jax.shard_map(
        on_device, mesh=mesh, in_specs=placed, out_specs=P("ma", "blk", None, None), check_vma=False
    )
```
